32 devices in a mesh: horiz: 16 (over z, y, core), vert: 2 (over x).
Axes of the slice: x: 2, y: 2, z: 4, core: 2. Of those that a mesh axis runs over, the one named last changes fastest.
Arguments:
- right_side: float32 [32, 64, 4096], P('vert', None, 'horiz'), may hold values from -6 to 6
- neighbours: int32 [4, 4096], P(None, 'horiz'), may hold values from 0 to 4095, as said below
- ocean_count: int32 [16], P('horiz'), may hold values from 64 to 256, as said below
- settling: float32 [32, 64], replicated, may hold values from 0.2 to 544
- coupling: float32 [32, 64, 64], P('vert'), may hold values from -0.3 to 0.3
- precond_inverse: float32 [32, 64, 64], P('vert'), may hold values from -1 to 1
Outputs:
- solution: float32 [32, 64, 4096], P('vert', None, 'horiz')
- residual: float32 [32, 64, 4096], P('vert', None, 'horiz')
The draws below stay inside these ranges and needn't reach their ends.
Inputs may be any that keep to these rules, and one draw needn't show every extreme that they name: Each column's neighbours lie within 256 columns of it in the global order; in every tile but the first some column reads the column that lies 256 - 1 columns before the tile's first one, and the first column reads the column just before it; in every tile but the last some column reads the column that lies 256 - 1 columns after the tile's last one, and the last column reads the column just after it. Tile t has ocean_count[t] ocean columns, the first half (rounded up) at its start and the rest at its end; some tile is all ocean.
All inputs are finite; a program needn't handle non-finite values.
Results may differ from the reference program's by a relative error of at most 0.00018.
Values sent between devices are 32-bit elements; how exact they have to be, the bound alone decides.
A program may use at most 64 MiB of HBM per device.

```python
import math
import jax
import jax.numpy as jnp
from jax import lax

CLASSES = 64
COLS_DEV = 256
RIM = 256
NB = 4
DEPTH_LEVELS = 32
COLUMNS = 4096
TILES = 16


VERT_DIFFUSION = 0.5


HORIZ_DIFFUSION = 0.25


def class_coefficients(key):
    key_perm = jax.random.fold_in(key, 101)
    key_slow = jax.random.fold_in(key, 102)
    key_fast = jax.random.fold_in(key, 103)
    key_factor = jax.random.fold_in(key, 104)
    first_subkey = jax.random.fold_in(key, 105)
    second_subkey = jax.random.fold_in(key, 106)
    key_couple = jax.random.fold_in(key, 107)
    order = jax.random.permutation(key_perm, CLASSES)
    slower_class = order < CLASSES // 2
    coupled = jnp.clip(jax.random.normal(key_couple, (DEPTH_LEVELS, CLASSES, CLASSES), jnp.float32), -4.0, 4.0) * (0.6 / math.sqrt(CLASSES))
    slow_base = jnp.exp(jax.random.uniform(key_slow, (CLASSES,), jnp.float32, math.log(6.0 * DEPTH_LEVELS), math.log(12.0 * DEPTH_LEVELS)))
    fast_base = jnp.exp(jax.random.uniform(key_fast, (CLASSES,), jnp.float32, math.log(0.3), math.log(3.0)))
    settling_base_rate = jnp.where(slower_class, slow_base, fast_base)
    multiplier = jnp.exp(jax.random.uniform(key_factor, (DEPTH_LEVELS, CLASSES), jnp.float32, math.log(0.7), math.log(1.4)))
    depth_level_index = jnp.arange(DEPTH_LEVELS, dtype=jnp.int32)[:, None]
    first_pulse = jax.random.randint(first_subkey, (), 1, DEPTH_LEVELS)
    second_pulse = jax.random.randint(second_subkey, (), 1, DEPTH_LEVELS)
    pulse_events = (depth_level_index == first_pulse) | (depth_level_index == second_pulse)
    settling = jnp.where(pulse_events & slower_class[None, :], 3.0 * multiplier, settling_base_rate[None, :] * multiplier)
    diagonal = 1.0 + settling + 2.0 * VERT_DIFFUSION + NB * HORIZ_DIFFUSION
    identity = jnp.eye(CLASSES, dtype=jnp.float32)[None]
    inverse = identity / diagonal[:, :, None] - coupled / (diagonal[:, :, None] * diagonal[:, None, :])
    return (settling, coupled, inverse)


def draw_settling(key, part):
    return class_coefficients(key)[0]


def draw_coupling(key, part):
    return class_coefficients(key)[1]


def draw_precond_inverse(key, part):
    return class_coefficients(key)[2]


def draw_ocean_count(key, part):
    key_counts = jax.random.fold_in(key, 201)
    key_full = jax.random.fold_in(key, 202)
    counts = jax.random.randint(key_counts, (TILES,), COLS_DEV // 4, COLS_DEV + 1)
    full_tile = jax.random.randint(key_full, (), 0, TILES)
    return jnp.where(jnp.arange(TILES, dtype=jnp.int32) == full_tile, COLS_DEV, counts).astype(jnp.int32)


def draw_neighbours(key, part):
    key_offset = jax.random.fold_in(key, 301)
    key_low = jax.random.fold_in(key, 302)
    key_high = jax.random.fold_in(key, 303)
    column = jnp.arange(COLUMNS, dtype=jnp.int32)
    offset = jax.random.randint(key_offset, (NB, COLUMNS), -RIM, RIM + 1)
    chosen = column[None, :] + offset
    inside = column % COLS_DEV
    tile_index = column // COLS_DEV
    slot_low = jax.random.randint(key_low, (TILES,), 0, NB)
    slot_high = jax.random.randint(key_high, (TILES,), 0, NB)
    near_low = (slot_low + 1) % NB
    near_high = (slot_high + 1) % NB
    slot_rows = jnp.arange(NB, dtype=jnp.int32)[:, None]
    low_hit = (inside == 1)[None, :] & (slot_rows == slot_low[tile_index][None, :])
    high_hit = (inside == COLS_DEV - 2)[None, :] & (slot_rows == slot_high[tile_index][None, :])
    edge_low = (inside == 0)[None, :] & (slot_rows == near_low[tile_index][None, :])
    edge_high = (inside == COLS_DEV - 1)[None, :] & (slot_rows == near_high[tile_index][None, :])
    chosen = jnp.where(low_hit, column[None, :] - 1 - RIM, chosen)
    chosen = jnp.where(high_hit, column[None, :] + 1 + RIM, chosen)
    chosen = jnp.where(edge_low, column[None, :] - 1, chosen)
    chosen = jnp.where(edge_high, column[None, :] + 1, chosen)
    chosen = jnp.where(low_hit | high_hit, jnp.clip(chosen, column[None, :] - RIM, column[None, :] + RIM), chosen)
    return jnp.clip(chosen, 0, COLUMNS - 1).astype(jnp.int32)


def level_of(rng, extent, shards, low, largest):
    gain = 1.0
    for axis_at, blocks in shards:
        draws = jax.random.uniform(jax.random.fold_in(jax.random.fold_in(rng, 6), axis_at), (blocks,), jnp.float32, low / len(shards), largest / len(shards))
        gain = gain * jnp.repeat(jnp.exp(draws), extent[axis_at] // blocks).reshape((-1,) + (1,) * (len(extent) - 1 - axis_at))
    return gain


def scatter_about(rng, shape, width, most, split=(), held_as=jnp.bfloat16):
    array = jax.random.normal(rng, shape, jnp.float32) * width
    if len(split) > 0:
        array = level_of(rng, shape, split, -0.22, 0.18) * array
    return jnp.clip(array, min=-most, max=most).astype(held_as)


def setup_inputs(seed: int = 0) -> dict:
    keys = jax.random.split(jax.random.key(seed), 7)
    return {
        "right_side": scatter_about(keys[0], (DEPTH_LEVELS, CLASSES, COLUMNS), 1.0, 6.0, ((0, 2), (2, 16)), jnp.float32),
        "neighbours": draw_neighbours(jax.random.fold_in(keys[6], 71), 0),
        "ocean_count": draw_ocean_count(jax.random.fold_in(keys[6], 71), 0),
        "settling": draw_settling(jax.random.fold_in(keys[6], 71), 0),
        "coupling": draw_coupling(jax.random.fold_in(keys[6], 71), 0),
        "precond_inverse": draw_precond_inverse(jax.random.fold_in(keys[6], 71), 0),
    }


VERT_DIFFUSION = 0.5
HORIZ_DIFFUSION = 0.25
CENTER_VALUE = 1.0
HALF_WIDTH = 0.6


def ocean_of(ocean_count):
    column = jnp.arange(COLUMNS, dtype=jnp.int32)
    inside = column % COLS_DEV
    tile_index = column // COLS_DEV
    count_here = ocean_count[tile_index]
    lower_part = (count_here + 1) // 2
    upper_part = count_here // 2
    return ((inside < lower_part) | (inside >= COLS_DEV - upper_part)).astype(jnp.float32)


def operate(field, settling, coupling, neighbours, ocean_mask, inflow_rate):
    diagonal = 1.0 + settling + 2.0 * VERT_DIFFUSION + NB * HORIZ_DIFFUSION
    coupled = jnp.einsum("kij,kjc->kic", coupling, field, precision=lax.Precision.HIGHEST)
    zero_level = jnp.zeros_like(field[:1])
    above_level = jnp.concatenate([zero_level, field[:-1]], axis=0)
    below_level = jnp.concatenate([field[1:], zero_level], axis=0)
    horizontal = jnp.zeros_like(field)
    for neighbour_slot in range(NB):
        horizontal = horizontal + jnp.take(field, neighbours[neighbour_slot], axis=2)
    total = (diagonal[:, :, None] * field + coupled - inflow_rate[:, :, None] * above_level
             - VERT_DIFFUSION * below_level - HORIZ_DIFFUSION * horizontal)
    return ocean_mask[None, None, :] * total


def column_sweep(residual, blocks, inflow_rate):
    def one_level(previous, pieces):
        resid_level, block, rate = pieces
        current = jnp.dot(block, resid_level + rate[:, None] * previous, precision=lax.Precision.HIGHEST)
        return current, current

    _, swept = lax.scan(one_level, jnp.zeros_like(residual[0]), (residual, blocks, inflow_rate))
    return swept


def reference(right_side, neighbours, ocean_count, settling, coupling, precond_inverse):
    ocean_mask = ocean_of(ocean_count)
    inflow_rate = jnp.concatenate([jnp.zeros_like(settling[:1]), settling[:-1]], axis=0) + VERT_DIFFUSION
    source = right_side * ocean_mask[None, None, :]
    spread_ratio = CENTER_VALUE / HALF_WIDTH
    ratio_first = 1.0 / spread_ratio
    ratio_second = 1.0 / (2.0 * spread_ratio - ratio_first)
    first_step = column_sweep(source, precond_inverse, inflow_rate) / CENTER_VALUE
    middle_residual = source - operate(first_step, settling, coupling, neighbours, ocean_mask, inflow_rate)
    second_precond = column_sweep(middle_residual, precond_inverse, inflow_rate)
    second_step = ratio_second * ratio_first * first_step + (2.0 * ratio_second / HALF_WIDTH) * second_precond
    solution = first_step + second_step
    residual = middle_residual - operate(second_step, settling, coupling, neighbours, ocean_mask, inflow_rate)
    return solution, residual
```

```python
import jax
import jax.numpy as jnp
from jax import lax
from jax.experimental import pallas as pl
from jax.experimental.pallas import tpu as pltpu
from jax.sharding import PartitionSpec as P

VERT_DIFFUSION = 0.5
HORIZ_DIFFUSION = 0.25
HALF_WIDTH = 0.6
NB = 4
SPREAD = 1.0 / HALF_WIDTH
RATIO_FIRST = 1.0 / SPREAD
RATIO_SECOND = 1.0 / (2.0 * SPREAD - RATIO_FIRST)
CA = RATIO_SECOND * RATIO_FIRST
CB = 2.0 * RATIO_SECOND / HALF_WIDTH

F32 = jnp.float32
BF = jnp.bfloat16
CHUNKS = 4


def split(x):
    hi = x.astype(BF)
    return hi, (x - hi.astype(F32)).astype(BF)


def mm(a, b):
    return jnp.dot(a, b, preferred_element_type=F32)


def mm3(ahi, alo, bhi, blo):
    return mm(ahi, bhi) + mm(ahi, blo) + mm(alo, bhi)


def make_kernel(tiles, slabs, levels, classes, cols):
    rows = levels * classes
    part = rows // CHUNKS
    block = 256

    def kernel(rhs, nbr, count, binv, coup, rate_row, diag, rate, sol, res,
               win, info, info_adj, h1, g_own, g_adj, phi, plo, xhi, xlo, fbuf, fout, mid,
               pbuf, pout, sbuf,
               recv, send_mate, send_direct, send_fwd, info_s, info_r, h_s, h_r, v_s, v_r):
        t = lax.axis_index("horiz")
        v = lax.axis_index("vert")
        c = lax.rem(t, 2)
        j = lax.div(t, 2)
        odd = lax.rem(j, 2)
        inner = lax.rem(j + c, 2) == 1
        own = 2 - c
        mate_pos = 3 - 3 * c
        mate = t + 1 - 2 * c
        direct = jnp.where(odd == 0, 2 * j + 2, 2 * j - 1)
        fwd = jnp.where(odd == 0, 2 * j + 4, 2 * j - 3)
        has_fwd = jnp.logical_and(inner, jnp.logical_and(fwd >= 0, fwd < tiles))
        adj = t - 1 + 2 * c
        has_adj = jnp.logical_and(adj >= 0, adj < tiles)
        first_slab = v == 0
        last_slab = v == slabs - 1

        def remote(src, dst, s, r, to):
            return pltpu.make_async_remote_copy(
                src_ref=src, dst_ref=dst, send_sem=s, recv_sem=r, device_id=to,
                device_id_type=pl.DeviceIdType.MESH)

        def piece(pos, ch):
            return win.at[pos, pl.ds(ch * part, part)]

        inside = lax.broadcasted_iota(jnp.int32, (1, cols), 1)
        n = count[0]
        low = lax.div(n + 1, 2)
        high = cols - lax.div(n, 2)
        ocean = jnp.logical_or(inside < low, inside >= high)
        ocean_i = ocean.astype(jnp.int32)
        ocean_f = ocean.astype(F32)
        info[...] = jnp.concatenate([nbr[...], jnp.broadcast_to(ocean_i, (4, cols))], axis=0)
        adj_copy = remote(info, info_adj, info_s, info_r, {"horiz": adj})

        @pl.when(has_adj)
        def _():
            adj_copy.start()

        directs = []
        for ch in range(CHUNKS):
            r = pl.ds(ch * part, part)
            win[own, r] = rhs[r] * ocean_f
            cp = remote(piece(own, ch), piece(c + 2 * odd, ch), send_direct.at[ch],
                        recv.at[c + 2 * odd, ch], {"horiz": direct})
            cp.start()
            directs.append(cp)
        mates = []
        for ch in range(CHUNKS):
            cp = remote(piece(own, ch), piece(3 * c, ch), send_mate.at[ch],
                        recv.at[3 * c, ch], {"horiz": mate})
            cp.start()
            mates.append(cp)

        @pl.when(jnp.logical_not(has_adj))
        def _():
            info_adj[...] = jnp.zeros_like(info_adj)
            win[2 * c] = jnp.zeros((rows, cols), F32)
            win[2 * c + 1] = jnp.zeros((rows, cols), F32)

        @pl.when(first_slab)
        def _():
            fbuf[0:classes] = jnp.zeros((classes, 3 * cols), F32)
            pbuf[0:classes] = jnp.zeros((classes, 2 * cols), F32)

        @pl.when(last_slab)
        def _():
            fbuf[classes + rows:] = jnp.zeros((classes, 3 * cols), F32)
            pbuf[classes + rows:] = jnp.zeros((classes, 2 * cols), F32)

        def fwd_copy(i, ch):
            return remote(piece(2 * c + i, ch), piece(2 * (1 - c) + i, ch), send_fwd.at[i, ch],
                          recv.at[2 * (1 - c) + i, ch], {"horiz": fwd})

        def arrive(ch):
            for i in range(2):
                @pl.when(has_adj)
                def _():
                    remote(piece(2 * c + i, ch), piece(2 * c + i, ch), send_fwd.at[i, ch],
                           recv.at[2 * c + i, ch], {"horiz": mate}).wait_recv()

                @pl.when(has_fwd)
                def _():
                    fwd_copy(i, ch).start()

        def build(dst, source, tile):
            base = (tile - 1) * cols
            mask = source[4:5].astype(F32)
            for b in range(3):
                at = lax.broadcasted_iota(jnp.int32, (cols, cols), 0) + (base + b * cols)
                total = jnp.zeros((cols, cols), F32)
                for q in range(NB):
                    total = total + jnp.where(at == source[q:q + 1], 1.0, 0.0)
                dst[b * cols:(b + 1) * cols] = (total * mask).astype(BF)

        build(g_own, info, t)

        wide = rows + 2 * classes
        lane = lax.broadcasted_iota(jnp.int32, (classes, wide), 1)
        row = lax.broadcasted_iota(jnp.int32, (classes, wide), 0)
        prev = jnp.where(lane == row + rows, 1.0, 0.0)

        def level_of_matrix(k, prev):
            bk = binv[k]
            mhi, mlo = split(bk[:, :classes] * rate_row[k])
            qhi, qlo = split(prev)
            new = mm3(mhi, mlo, qhi, qlo)
            both = jnp.concatenate([bk] * (wide // (2 * classes)), axis=1)
            new = new + jnp.where(lax.div(lane, classes) == k, both, 0.0)
            nhi, nlo = split(new)
            phi[pl.ds(pl.multiple_of(k * classes, classes), classes)] = nhi
            plo[pl.ds(pl.multiple_of(k * classes, classes), classes)] = nlo
            return new

        for ch in range(CHUNKS):
            lo = ch * (levels // CHUNKS)
            prev = lax.fori_loop(lo, lo + levels // CHUNKS, level_of_matrix, prev)
            arrive(ch)

        @pl.when(has_adj)
        def _():
            adj_copy.wait_recv()

        build(g_adj, info_adj, adj)
        for ch in range(CHUNKS):
            remote(piece(mate_pos, ch), piece(mate_pos, ch), send_mate.at[ch],
                   recv.at[mate_pos, ch], {"horiz": mate}).wait_recv()

        def gather(src, first, g, r):
            out = jnp.zeros((block, cols), F32)
            for b in range(3):
                hi, lo = split(src[first + b, r])
                gb = g[b * cols:(b + 1) * cols]
                out = out + mm(hi, gb) + mm(lo, gb)
            return out

        def put_x(r, s, value):
            hi, lo = split(value)
            xhi[r, s * cols:(s + 1) * cols] = hi
            xlo[r, s * cols:(s + 1) * cols] = lo

        def blocks(fn):
            def step(i, carry):
                fn(pl.ds(pl.multiple_of(i * block, block), block))
                return carry
            lax.fori_loop(0, rows // block, step, 0)

        def own_first(r):
            value = gather(win, own - 1, g_own, r)
            h1[1, r] = value
            put_x(r, 0, win[own, r])
            put_x(r, 1, value)

        blocks(own_first)
        h_copy = remote(h1.at[1], h1.at[2 * c], h_s, h_r, {"horiz": mate})
        h_copy.start()

        def adj_first(r):
            h1[2 * c, r] = gather(win, c, g_adj, r)

        def second_sum(r):
            put_x(r, 2, gather(h1, 0, g_own, r))

        h_slot = 2 - 2 * c
        h_adj = 2 * c
        del h_slot, h_adj
        blocks(adj_first)
        h_copy.wait_recv()
        blocks(second_sum)

        def sweep(x_cols, buf, out, up_cols, sem):
            down = remote(out, buf.at[0:classes], v_s.at[sem], v_r.at[sem], {"vert": v + 1})
            up = remote(buf.at[classes:2 * classes, 0:up_cols],
                        buf.at[classes + rows:2 * classes + rows, 0:up_cols],
                        v_s.at[sem + 1], v_r.at[sem + 1], {"vert": v - 1})
            tail = slice(rows - classes, rows)
            last = mm3(phi[tail, :rows], plo[tail, :rows], xhi[:, :x_cols], xlo[:, :x_cols])
            out[...] = last

            @pl.when(jnp.logical_and(first_slab, slabs > 1))
            def _():
                down.start()

            for b in range(rows // block):
                r = slice(b * block, (b + 1) * block)
                k = slice(0, (b + 1) * block)
                buf[classes + b * block:classes + (b + 1) * block] = mm3(
                    phi[r, k], plo[r, k], xhi[k, :x_cols], xlo[k, :x_cols])

            @pl.when(jnp.logical_not(first_slab))
            def _():
                down.wait_recv()
                ihi, ilo = split(buf[0:classes])
                ti = slice(rows, rows + classes)
                out[...] = out[...] + mm3(phi[tail, ti], plo[tail, ti], ihi, ilo)

                @pl.when(jnp.logical_not(last_slab))
                def _():
                    down.start()

                for b in range(rows // block):
                    r = slice(b * block, (b + 1) * block)
                    br = slice(classes + b * block, classes + (b + 1) * block)
                    buf[br] = buf[br] + mm3(phi[r, ti], plo[r, ti], ihi, ilo)
                    if b == 0:
                        up.start()

            @pl.when(jnp.logical_not(last_slab))
            def _():
                up.wait_recv()
                down.wait_send()

            @pl.when(jnp.logical_not(first_slab))
            def _():
                up.wait_send()

        def operate(k, buf, width):
            at = pl.multiple_of(k * classes, classes)
            here = buf[pl.ds(at + classes, classes), 0:width]
            above = buf[pl.ds(at, classes), 0:width]
            below = buf[pl.ds(at + 2 * classes, classes), 0:width]
            chi, clo = split(coup[k])
            hhi, hlo = split(here)
            reps = width // 128
            d = jnp.concatenate([diag[pl.ds(at, classes)]] * reps, axis=1)
            ra = jnp.concatenate([rate[pl.ds(at, classes)]] * reps, axis=1)
            return (d * here + mm3(chi, clo, hhi, hlo) - ra * above - VERT_DIFFUSION * below)

        sweep(3 * cols, fbuf, fout, 2 * cols, 0)

        def middle(k, carry):
            r = pl.ds(pl.multiple_of(k * classes, classes), classes)
            rf = pl.ds(pl.multiple_of(k * classes + classes, classes), classes)
            lf = operate(k, fbuf, 2 * cols)
            m = win[own, r] - lf[:, :cols] + HORIZ_DIFFUSION * fbuf[rf, cols:2 * cols]
            hm = h1[1, r] - lf[:, cols:] + HORIZ_DIFFUSION * fbuf[rf, 2 * cols:3 * cols]
            mid[r] = m
            put_x(r, 0, m)
            put_x(r, 1, hm)
            return carry

        lax.fori_loop(0, levels, middle, 0)
        sweep(2 * cols, pbuf, pout, cols, 2)
        sbuf[...] = CA * fbuf[:, 0:cols] + CB * pbuf[:, 0:cols]

        def final(k, carry):
            r = pl.ds(pl.multiple_of(k * classes, classes), classes)
            rf = pl.ds(pl.multiple_of(k * classes + classes, classes), classes)
            hs = CA * fbuf[rf, cols:2 * cols] + CB * pbuf[rf, cols:2 * cols]
            sol[r] = fbuf[rf, 0:cols] + sbuf[rf]
            res[r] = mid[r] - operate(k, sbuf, cols) + HORIZ_DIFFUSION * hs
            return carry

        lax.fori_loop(0, levels, final, 0)

        for cp in directs + mates:
            cp.wait_send()
        h_copy.wait_send()

        @pl.when(has_adj)
        def _():
            adj_copy.wait_send()

        @pl.when(has_fwd)
        def _():
            for ch in range(CHUNKS):
                for i in range(2):
                    fwd_copy(i, ch).wait_send()

    return kernel


def solution(mesh):
    tiles, slabs = mesh.shape["horiz"], mesh.shape["vert"]

    def body(right_side, neighbours, ocean_count, settling, coupling, precond_inverse):
        levels, classes, cols = right_side.shape
        rows = levels * classes
        start = lax.axis_index("vert") * levels
        inflow = jnp.concatenate([jnp.zeros_like(settling[:1]), settling[:-1]], 0) + VERT_DIFFUSION
        rate = lax.dynamic_slice_in_dim(inflow, start, levels, 0)
        diag = (1.0 + lax.dynamic_slice_in_dim(settling, start, levels, 0)
                + 2.0 * VERT_DIFFUSION + NB * HORIZ_DIFFUSION)
        twice = jnp.concatenate([precond_inverse] * 2, axis=2)
        spread = lambda x: jnp.broadcast_to(x.reshape(rows, 1), (rows, 128))
        vm = pl.BlockSpec(memory_space=pltpu.VMEM)
        dma = pltpu.SemaphoreType.DMA
        wide = rows + 2 * classes
        sol, res = pl.pallas_call(
            make_kernel(tiles, slabs, levels, classes, cols),
            out_shape=[jax.ShapeDtypeStruct((rows, cols), F32)] * 2,
            in_specs=[vm, vm, pl.BlockSpec(memory_space=pltpu.SMEM)] + [vm] * 5,
            out_specs=[vm, vm],
            scratch_shapes=[
                pltpu.VMEM((4, rows, cols), F32),
                pltpu.VMEM((8, cols), jnp.int32),
                pltpu.VMEM((8, cols), jnp.int32),
                pltpu.VMEM((3, rows, cols), F32),
                pltpu.VMEM((3 * cols, cols), BF),
                pltpu.VMEM((3 * cols, cols), BF),
                pltpu.VMEM((rows, wide), BF),
                pltpu.VMEM((rows, wide), BF),
                pltpu.VMEM((rows, 3 * cols), BF),
                pltpu.VMEM((rows, 3 * cols), BF),
                pltpu.VMEM((rows + 2 * classes, 3 * cols), F32),
                pltpu.VMEM((classes, 3 * cols), F32),
                pltpu.VMEM((rows, cols), F32),
                pltpu.VMEM((rows + 2 * classes, 2 * cols), F32),
                pltpu.VMEM((classes, 2 * cols), F32),
                pltpu.VMEM((rows + 2 * classes, cols), F32),
                dma((4, CHUNKS)), dma((CHUNKS,)), dma((CHUNKS,)), dma((2, CHUNKS)),
                dma, dma, dma, dma, dma((4,)), dma((4,)),
            ],
            compiler_params=pltpu.CompilerParams(
                has_side_effects=True, vmem_limit_bytes=56 * 2**20),
            name="settle",
        )(right_side.reshape(rows, cols), neighbours, ocean_count, twice, coupling,
          rate.reshape(levels, 1, classes), spread(diag), spread(rate))
        return sol.reshape(right_side.shape), res.reshape(right_side.shape)

    in_specs = (P("vert", None, "horiz"), P(None, "horiz"), P("horiz"), P(),
                P("vert", None, None), P("vert", None, None))
    out_specs = (P("vert", None, "horiz"), P("vert", None, "horiz"))
    return jax.shard_map(body, mesh=mesh, in_specs=in_specs, out_specs=out_specs, check_vma=False)
```

```python
import jax
import jax.numpy as jnp
from jax import lax
from jax.experimental import pallas as pl
from jax.experimental.pallas import tpu as pltpu
from jax.sharding import PartitionSpec as P

VERT_DIFFUSION = 0.5
HORIZ_DIFFUSION = 0.25
HALF_WIDTH = 0.6
NB = 4
SPREAD = 1.0 / HALF_WIDTH
RATIO_FIRST = 1.0 / SPREAD
RATIO_SECOND = 1.0 / (2.0 * SPREAD - RATIO_FIRST)
CA = RATIO_SECOND * RATIO_FIRST
CB = 2.0 * RATIO_SECOND / HALF_WIDTH

F32 = jnp.float32
BF = jnp.bfloat16
CHUNKS = 8


def split(x):
    hi = x.astype(BF)
    return hi, (x - hi.astype(F32)).astype(BF)


def mm(a, b):
    return jnp.dot(a, b, preferred_element_type=F32)


def mm3(ahi, alo, bhi, blo):
    return mm(ahi, bhi) + mm(ahi, blo) + mm(alo, bhi)


def make_kernel(tiles, slabs, levels, classes, cols):
    rows = levels * classes
    part = rows // CHUNKS
    block = 256

    def kernel(rhs, nbr, count, settling, coup, binv, sol, res,
               win, info, info_adj, h1, g_own, g_adj, phi, plo, xhi, xlo, fbuf, fout, mid,
               pbuf, pout, sbuf,
               recv, send_mate, send_direct, send_fwd, info_s, info_r, h_s, h_r, v_s, v_r):
        t = lax.axis_index("horiz")
        v = lax.axis_index("vert")
        c = lax.rem(t, 2)
        j = lax.div(t, 2)
        odd = lax.rem(j, 2)
        inner = lax.rem(j + c, 2) == 1
        own = 2 - c
        mate_pos = 3 - 3 * c
        mate = t + 1 - 2 * c
        direct = jnp.where(odd == 0, 2 * j + 2, 2 * j - 1)
        fwd = jnp.where(odd == 0, 2 * j + 4, 2 * j - 3)
        has_fwd = jnp.logical_and(inner, jnp.logical_and(fwd >= 0, fwd < tiles))
        adj = t - 1 + 2 * c
        has_adj = jnp.logical_and(adj >= 0, adj < tiles)
        first_slab = v == 0
        last_slab = v == slabs - 1

        def remote(src, dst, s, r, to):
            return pltpu.make_async_remote_copy(
                src_ref=src, dst_ref=dst, send_sem=s, recv_sem=r, device_id=to,
                device_id_type=pl.DeviceIdType.MESH)

        def piece(pos, ch):
            return win.at[pos, pl.ds(ch * part, part)]

        pj = j + 1 - 2 * odd
        partner_inner = direct
        partner_outer = 4 * pj + 1 - direct
        outer = jnp.logical_not(inner)
        from_fwd = jnp.where(odd == 0, 2 * j - 3, 2 * j + 4)
        outer_adj = jnp.logical_and(outer, has_adj)
        barrier = pltpu.get_barrier_semaphore()

        def greet(to):
            pl.semaphore_signal(barrier, inc=1, device_id=to, device_id_type=pl.DeviceIdType.MESH)

        greet({"horiz": mate})
        greet({"horiz": partner_inner})

        @pl.when(inner)
        def _():
            greet({"horiz": partner_outer})

        @pl.when(has_fwd)
        def _():
            greet({"horiz": fwd})

        @pl.when(outer_adj)
        def _():
            greet({"horiz": from_fwd})
            greet({"horiz": adj})

        @pl.when(jnp.logical_not(first_slab))
        def _():
            greet({"vert": v - 1})

        @pl.when(jnp.logical_not(last_slab))
        def _():
            greet({"vert": v + 1})

        greeted = (2 + jnp.where(inner, 1, 0) + jnp.where(has_fwd, 1, 0)
                   + jnp.where(outer_adj, 2, 0) + jnp.where(first_slab, 0, 1)
                   + jnp.where(last_slab, 0, 1))

        inside = lax.broadcasted_iota(jnp.int32, (1, cols), 1)
        n = count[0]
        low = lax.div(n + 1, 2)
        high = cols - lax.div(n, 2)
        ocean = jnp.logical_or(inside < low, inside >= high)
        ocean_i = ocean.astype(jnp.int32)
        ocean_f = ocean.astype(F32)
        info[...] = jnp.concatenate([nbr[...], jnp.broadcast_to(ocean_i, (4, cols))], axis=0)
        for ch in range(CHUNKS):
            r = pl.ds(ch * part, part)
            win[own, r] = rhs[r] * ocean_f
        pl.semaphore_wait(barrier, greeted)
        adj_copy = remote(info, info_adj, info_s, info_r, {"horiz": adj})

        @pl.when(has_adj)
        def _():
            adj_copy.start()

        directs = []
        for ch in range(CHUNKS):
            cp = remote(piece(own, ch), piece(c + 2 * odd, ch), send_direct.at[ch],
                        recv.at[c + 2 * odd, ch], {"horiz": direct})
            cp.start()
            directs.append(cp)
        mates = []
        for ch in range(CHUNKS):
            cp = remote(piece(own, ch), piece(3 * c, ch), send_mate.at[ch],
                        recv.at[3 * c, ch], {"horiz": mate})
            cp.start()
            mates.append(cp)

        @pl.when(jnp.logical_not(has_adj))
        def _():
            info_adj[...] = jnp.zeros_like(info_adj)
            win[2 * c] = jnp.zeros((rows, cols), F32)
            win[2 * c + 1] = jnp.zeros((rows, cols), F32)

        @pl.when(first_slab)
        def _():
            fbuf[0:classes] = jnp.zeros((classes, 3 * cols), F32)
            pbuf[0:classes] = jnp.zeros((classes, 2 * cols), F32)

        @pl.when(last_slab)
        def _():
            fbuf[classes + rows:] = jnp.zeros((classes, 3 * cols), F32)
            pbuf[classes + rows:] = jnp.zeros((classes, 2 * cols), F32)

        def fwd_copy(i, ch):
            return remote(piece(2 * c + i, ch), piece(2 * (1 - c) + i, ch), send_fwd.at[i, ch],
                          recv.at[2 * (1 - c) + i, ch], {"horiz": fwd})

        def arrive(ch):
            for i in range(2):
                @pl.when(has_adj)
                def _():
                    remote(piece(2 * c + i, ch), piece(2 * c + i, ch), send_fwd.at[i, ch],
                           recv.at[2 * c + i, ch], {"horiz": mate}).wait_recv()

                @pl.when(has_fwd)
                def _():
                    fwd_copy(i, ch).start()

        def build(dst, source, tile):
            base = (tile - 1) * cols
            mask = source[4:5].astype(F32)
            for b in range(3):
                at = lax.broadcasted_iota(jnp.int32, (cols, cols), 0) + (base + b * cols)
                total = jnp.zeros((cols, cols), F32)
                for q in range(NB):
                    total = total + jnp.where(at == source[q:q + 1], 1.0, 0.0)
                dst[b * cols:(b + 1) * cols] = (total * mask).astype(BF)

        build(g_own, info, t)

        eye = (lax.broadcasted_iota(jnp.int32, (classes, classes), 0)
               == lax.broadcasted_iota(jnp.int32, (classes, classes), 1))

        def rate_of(k):
            level = v * levels + k
            above = settling[pl.ds(jnp.maximum(level - 1, 0), 1)]
            return jnp.where(level > 0, above, 0.0) + VERT_DIFFUSION

        def diag_of(k):
            return (1.0 + settling[pl.ds(v * levels + k, 1)] + 2.0 * VERT_DIFFUSION
                    + NB * HORIZ_DIFFUSION)

        def column(x):
            return jnp.sum(jnp.where(eye, x, 0.0), axis=1, keepdims=True)

        wide = rows + 2 * classes
        lane = lax.broadcasted_iota(jnp.int32, (classes, wide), 1)
        row = lax.broadcasted_iota(jnp.int32, (classes, wide), 0)
        prev = jnp.where(lane == row + rows, 1.0, 0.0)

        def level_of_matrix(k, prev):
            bk = binv[k]
            mhi, mlo = split(bk * rate_of(k))
            qhi, qlo = split(prev)
            new = mm3(mhi, mlo, qhi, qlo)
            both = jnp.concatenate([bk, bk], axis=1)
            both = jnp.concatenate([both] * (wide // (2 * classes)), axis=1)
            new = new + jnp.where(lax.div(lane, classes) == k, both, 0.0)
            nhi, nlo = split(new)
            phi[pl.ds(pl.multiple_of(k * classes, classes), classes)] = nhi
            plo[pl.ds(pl.multiple_of(k * classes, classes), classes)] = nlo
            return new

        lax.fori_loop(0, levels, level_of_matrix, prev)

        @pl.when(has_adj)
        def _():
            adj_copy.wait_recv()

        build(g_adj, info_adj, adj)

        def gather(src, first, g, r):
            out = jnp.zeros((block, cols), F32)
            for b in range(3):
                hi, lo = split(src[first + b, r])
                gb = g[b * cols:(b + 1) * cols]
                out = out + mm(hi, gb) + mm(lo, gb)
            return out

        def put_x(r, s, value):
            hi, lo = split(value)
            xhi[r, s * cols:(s + 1) * cols] = hi
            xlo[r, s * cols:(s + 1) * cols] = lo

        tail = slice(rows - classes, rows)
        ti = slice(rows, rows + classes)
        n_blocks = rows // block

        def first_sums(b):
            r = slice(b * block, (b + 1) * block)
            value = gather(win, own - 1, g_own, r)
            h1[1, r] = value
            put_x(r, 0, win[own, r])
            put_x(r, 1, value)
            h_copy[b].start()
            h1[2 * c, r] = gather(win, c, g_adj, r)

        def sweep_block(b, x_cols, buf):
            r = slice(b * block, (b + 1) * block)
            k = slice(0, (b + 1) * block)
            buf[classes + b * block:classes + (b + 1) * block] = mm3(
                phi[r, k], plo[r, k], xhi[k, :x_cols], xlo[k, :x_cols])

        def second_sums(b):
            r = slice(b * block, (b + 1) * block)
            h_copy[b].wait_recv()
            put_x(r, 2, gather(h1, 0, g_own, r))
            sweep_block(b, 3 * cols, fbuf)

        h_copy = []
        for b in range(n_blocks):
            r = pl.ds(b * block, block)
            h_copy.append(remote(h1.at[1, r], h1.at[2 * c, r], h_s.at[b], h_r.at[b],
                                 {"horiz": mate}))
        per = CHUNKS // n_blocks
        for b in range(n_blocks):
            for ch in range(b * per, (b + 1) * per):
                remote(piece(mate_pos, ch), piece(mate_pos, ch), send_mate.at[ch],
                       recv.at[mate_pos, ch], {"horiz": mate}).wait_recv()
                arrive(ch)
            first_sums(b)
            if b > 0:
                second_sums(b - 1)
        second_sums(n_blocks - 1)

        def relay(buf, out, up_cols, sem, rest):
            down = remote(out, buf.at[0:classes], v_s.at[sem], v_r.at[sem], {"vert": v + 1})
            up = remote(buf.at[classes:2 * classes, 0:up_cols],
                        buf.at[classes + rows:2 * classes + rows, 0:up_cols],
                        v_s.at[sem + 1], v_r.at[sem + 1], {"vert": v - 1})
            out[...] = buf[rows:rows + classes]

            @pl.when(jnp.logical_and(first_slab, slabs > 1))
            def _():
                down.start()

            rest()

            @pl.when(jnp.logical_not(first_slab))
            def _():
                down.wait_recv()
                ihi, ilo = split(buf[0:classes])
                out[...] = out[...] + mm3(phi[tail, ti], plo[tail, ti], ihi, ilo)

                @pl.when(jnp.logical_not(last_slab))
                def _():
                    down.start()

                for b in range(n_blocks):
                    r = slice(b * block, (b + 1) * block)
                    br = slice(classes + b * block, classes + (b + 1) * block)
                    buf[br] = buf[br] + mm3(phi[r, ti], plo[r, ti], ihi, ilo)
                    if b == 0:
                        up.start()

            @pl.when(jnp.logical_not(last_slab))
            def _():
                up.wait_recv()
                down.wait_send()

            @pl.when(jnp.logical_not(first_slab))
            def _():
                up.wait_send()

        def operate(k, buf, width):
            at = pl.multiple_of(k * classes, classes)
            here = buf[pl.ds(at + classes, classes), 0:width]
            above = buf[pl.ds(at, classes), 0:width]
            below = buf[pl.ds(at + 2 * classes, classes), 0:width]
            chi, clo = split(coup[k])
            hhi, hlo = split(here)
            d = column(diag_of(k))
            ra = column(rate_of(k))
            return (d * here + mm3(chi, clo, hhi, hlo) - ra * above - VERT_DIFFUSION * below)

        relay(fbuf, fout, 2 * cols, 0, lambda: None)

        def middle(k, carry):
            r = pl.ds(pl.multiple_of(k * classes, classes), classes)
            rf = pl.ds(pl.multiple_of(k * classes + classes, classes), classes)
            lf = operate(k, fbuf, 2 * cols)
            m = win[own, r] - lf[:, :cols] + HORIZ_DIFFUSION * fbuf[rf, cols:2 * cols]
            hm = h1[1, r] - lf[:, cols:] + HORIZ_DIFFUSION * fbuf[rf, 2 * cols:3 * cols]
            mid[r] = m
            put_x(r, 0, m)
            put_x(r, 1, hm)
            return carry

        def middles(i, carry):
            for u in range(4):
                middle(4 * i + u, carry)
            return carry

        lax.fori_loop(0, levels // 4, middles, 0)
        sweep_block(n_blocks - 1, 2 * cols, pbuf)

        def others():
            for b in range(n_blocks - 1):
                sweep_block(b, 2 * cols, pbuf)

        relay(pbuf, pout, cols, 2, others)
        sbuf[...] = CA * fbuf[:, 0:cols] + CB * pbuf[:, 0:cols]

        def final(k, carry):
            r = pl.ds(pl.multiple_of(k * classes, classes), classes)
            rf = pl.ds(pl.multiple_of(k * classes + classes, classes), classes)
            hs = CA * fbuf[rf, cols:2 * cols] + CB * pbuf[rf, cols:2 * cols]
            sol[r] = fbuf[rf, 0:cols] + sbuf[rf]
            res[r] = mid[r] - operate(k, sbuf, cols) + HORIZ_DIFFUSION * hs
            return carry

        def finals(i, carry):
            for u in range(4):
                final(4 * i + u, carry)
            return carry

        lax.fori_loop(0, levels // 4, finals, 0)

        for cp in directs + mates:
            cp.wait_send()
        for cp in h_copy:
            cp.wait_send()

        @pl.when(has_adj)
        def _():
            adj_copy.wait_send()

        @pl.when(has_fwd)
        def _():
            for ch in range(CHUNKS):
                for i in range(2):
                    fwd_copy(i, ch).wait_send()

    return kernel


def solution(mesh):
    tiles, slabs = mesh.shape["horiz"], mesh.shape["vert"]

    def body(right_side, neighbours, ocean_count, settling, coupling, precond_inverse):
        levels, classes, cols = right_side.shape
        rows = levels * classes
        vm = pl.BlockSpec(memory_space=pltpu.VMEM)
        dma = pltpu.SemaphoreType.DMA
        wide = rows + 2 * classes
        sol, res = pl.pallas_call(
            make_kernel(tiles, slabs, levels, classes, cols),
            out_shape=[jax.ShapeDtypeStruct((rows, cols), F32)] * 2,
            in_specs=[vm, vm, pl.BlockSpec(memory_space=pltpu.SMEM)] + [vm] * 3,
            out_specs=[vm, vm],
            scratch_shapes=[
                pltpu.VMEM((4, rows, cols), F32),
                pltpu.VMEM((8, cols), jnp.int32),
                pltpu.VMEM((8, cols), jnp.int32),
                pltpu.VMEM((3, rows, cols), F32),
                pltpu.VMEM((3 * cols, cols), BF),
                pltpu.VMEM((3 * cols, cols), BF),
                pltpu.VMEM((rows, wide), BF),
                pltpu.VMEM((rows, wide), BF),
                pltpu.VMEM((rows, 3 * cols), BF),
                pltpu.VMEM((rows, 3 * cols), BF),
                pltpu.VMEM((rows + 2 * classes, 3 * cols), F32),
                pltpu.VMEM((classes, 3 * cols), F32),
                pltpu.VMEM((rows, cols), F32),
                pltpu.VMEM((rows + 2 * classes, 2 * cols), F32),
                pltpu.VMEM((classes, 2 * cols), F32),
                pltpu.VMEM((rows + 2 * classes, cols), F32),
                dma((4, CHUNKS)), dma((CHUNKS,)), dma((CHUNKS,)), dma((2, CHUNKS)),
                dma, dma, dma((4,)), dma((4,)), dma((4,)), dma((4,)),
            ],
            compiler_params=pltpu.CompilerParams(
                collective_id=0, has_side_effects=True, vmem_limit_bytes=56 * 2**20),
            name="settle",
        )(right_side.reshape(rows, cols), neighbours, ocean_count, settling, coupling,
          precond_inverse)
        return sol.reshape(right_side.shape), res.reshape(right_side.shape)

    in_specs = (P("vert", None, "horiz"), P(None, "horiz"), P("horiz"), P(),
                P("vert", None, None), P("vert", None, None))
    out_specs = (P("vert", None, "horiz"), P("vert", None, "horiz"))
    return jax.shard_map(body, mesh=mesh, in_specs=in_specs, out_specs=out_specs, check_vma=False)
```

```python
import jax
import jax.numpy as jnp
from jax import lax
from jax.experimental import pallas as pl
from jax.experimental.pallas import tpu as pltpu
from jax.sharding import PartitionSpec as P

VERT_DIFFUSION = 0.5
HORIZ_DIFFUSION = 0.25
HALF_WIDTH = 0.6
NB = 4
SPREAD = 1.0 / HALF_WIDTH
RATIO_FIRST = 1.0 / SPREAD
RATIO_SECOND = 1.0 / (2.0 * SPREAD - RATIO_FIRST)
CA = RATIO_SECOND * RATIO_FIRST
CB = 2.0 * RATIO_SECOND / HALF_WIDTH

F32 = jnp.float32
BF = jnp.bfloat16
CHUNKS = 16


def split(x):
    hi = x.astype(BF)
    return hi, (x - hi.astype(F32)).astype(BF)


def mm(a, b):
    return jnp.dot(a, b, preferred_element_type=F32)


def mm3(ahi, alo, bhi, blo):
    return mm(ahi, bhi) + mm(ahi, blo) + mm(alo, bhi)


def make_kernel(tiles, slabs, levels, classes, cols):
    rows = levels * classes
    part = rows // CHUNKS
    block = 256

    def kernel(rhs, nbr, count, settling, coup, binv, sol, res,
               win, info, info_adj, h1, g_own, g_adj, phi, plo, xhi, xlo, fbuf, fout, mid,
               pbuf, pout, sbuf,
               recv, send_mate, send_direct, send_fwd, info_s, info_r, h_s, h_r, v_s, v_r):
        t = lax.axis_index("horiz")
        v = lax.axis_index("vert")
        c = lax.rem(t, 2)
        j = lax.div(t, 2)
        odd = lax.rem(j, 2)
        inner = lax.rem(j + c, 2) == 1
        own = 2 - c
        mate_pos = 3 - 3 * c
        mate = t + 1 - 2 * c
        direct = jnp.where(odd == 0, 2 * j + 2, 2 * j - 1)
        fwd = jnp.where(odd == 0, 2 * j + 4, 2 * j - 3)
        has_fwd = jnp.logical_and(inner, jnp.logical_and(fwd >= 0, fwd < tiles))
        adj = t - 1 + 2 * c
        has_adj = jnp.logical_and(adj >= 0, adj < tiles)
        first_slab = v == 0
        last_slab = v == slabs - 1

        def remote(src, dst, s, r, to):
            return pltpu.make_async_remote_copy(
                src_ref=src, dst_ref=dst, send_sem=s, recv_sem=r, device_id=to,
                device_id_type=pl.DeviceIdType.MESH)

        def piece(pos, ch):
            return win.at[pos, pl.ds(ch * part, part)]

        pj = j + 1 - 2 * odd
        partner_inner = direct
        partner_outer = 4 * pj + 1 - direct
        outer = jnp.logical_not(inner)
        from_fwd = jnp.where(odd == 0, 2 * j - 3, 2 * j + 4)
        outer_adj = jnp.logical_and(outer, has_adj)
        barrier = pltpu.get_barrier_semaphore()

        def greet(to):
            pl.semaphore_signal(barrier, inc=1, device_id=to, device_id_type=pl.DeviceIdType.MESH)

        greet({"horiz": mate})
        greet({"horiz": partner_inner})

        @pl.when(inner)
        def _():
            greet({"horiz": partner_outer})

        @pl.when(has_fwd)
        def _():
            greet({"horiz": fwd})

        @pl.when(outer_adj)
        def _():
            greet({"horiz": from_fwd})
            greet({"horiz": adj})

        @pl.when(jnp.logical_not(first_slab))
        def _():
            greet({"vert": v - 1})

        @pl.when(jnp.logical_not(last_slab))
        def _():
            greet({"vert": v + 1})

        greeted = (2 + jnp.where(inner, 1, 0) + jnp.where(has_fwd, 1, 0)
                   + jnp.where(outer_adj, 2, 0) + jnp.where(first_slab, 0, 1)
                   + jnp.where(last_slab, 0, 1))

        inside = lax.broadcasted_iota(jnp.int32, (1, cols), 1)
        n = count[0]
        low = lax.div(n + 1, 2)
        high = cols - lax.div(n, 2)
        ocean = jnp.logical_or(inside < low, inside >= high)
        ocean_i = ocean.astype(jnp.int32)
        ocean_f = ocean.astype(F32)
        info[...] = jnp.concatenate([nbr[...], jnp.broadcast_to(ocean_i, (4, cols))], axis=0)
        for ch in range(CHUNKS):
            r = pl.ds(ch * part, part)
            win[own, r] = rhs[r] * ocean_f
        pl.semaphore_wait(barrier, greeted)
        adj_copy = remote(info, info_adj, info_s, info_r, {"horiz": adj})

        @pl.when(has_adj)
        def _():
            adj_copy.start()

        directs = []
        for ch in range(CHUNKS):
            cp = remote(piece(own, ch), piece(c + 2 * odd, ch), send_direct.at[ch],
                        recv.at[c + 2 * odd, ch], {"horiz": direct})
            cp.start()
            directs.append(cp)
        mates = []
        for ch in range(CHUNKS):
            cp = remote(piece(own, ch), piece(3 * c, ch), send_mate.at[ch],
                        recv.at[3 * c, ch], {"horiz": mate})
            cp.start()
            mates.append(cp)

        @pl.when(jnp.logical_not(has_adj))
        def _():
            info_adj[...] = jnp.zeros_like(info_adj)
            win[2 * c] = jnp.zeros((rows, cols), F32)
            win[2 * c + 1] = jnp.zeros((rows, cols), F32)

        @pl.when(first_slab)
        def _():
            fbuf[0:classes] = jnp.zeros((classes, 3 * cols), F32)
            pbuf[0:classes] = jnp.zeros((classes, 2 * cols), F32)

        @pl.when(last_slab)
        def _():
            fbuf[classes + rows:] = jnp.zeros((classes, 3 * cols), F32)
            pbuf[classes + rows:] = jnp.zeros((classes, 2 * cols), F32)

        def fwd_copy(i, ch):
            return remote(piece(2 * c + i, ch), piece(2 * (1 - c) + i, ch), send_fwd.at[i, ch],
                          recv.at[2 * (1 - c) + i, ch], {"horiz": fwd})

        def arrive(ch):
            for i in range(2):
                @pl.when(has_adj)
                def _():
                    remote(piece(2 * c + i, ch), piece(2 * c + i, ch), send_fwd.at[i, ch],
                           recv.at[2 * c + i, ch], {"horiz": mate}).wait_recv()

                @pl.when(has_fwd)
                def _():
                    fwd_copy(i, ch).start()

        def build(dst, source, tile):
            base = (tile - 1) * cols
            mask = source[4:5].astype(F32)
            for b in range(3):
                at = lax.broadcasted_iota(jnp.int32, (cols, cols), 0) + (base + b * cols)
                total = jnp.zeros((cols, cols), F32)
                for q in range(NB):
                    total = total + jnp.where(at == source[q:q + 1], 1.0, 0.0)
                dst[b * cols:(b + 1) * cols] = (total * mask).astype(BF)

        build(g_own, info, t)

        eye = (lax.broadcasted_iota(jnp.int32, (classes, classes), 0)
               == lax.broadcasted_iota(jnp.int32, (classes, classes), 1))

        def rate_of(k):
            level = v * levels + k
            above = settling[pl.ds(jnp.maximum(level - 1, 0), 1)]
            return jnp.where(level > 0, above, 0.0) + VERT_DIFFUSION

        def diag_of(k):
            return (1.0 + settling[pl.ds(v * levels + k, 1)] + 2.0 * VERT_DIFFUSION
                    + NB * HORIZ_DIFFUSION)

        def column(x):
            return jnp.sum(jnp.where(eye, x, 0.0), axis=1, keepdims=True)

        wide = rows + 2 * classes
        lane = lax.broadcasted_iota(jnp.int32, (classes, wide), 1)
        row = lax.broadcasted_iota(jnp.int32, (classes, wide), 0)
        prev = jnp.where(lane == row + rows, 1.0, 0.0)

        def level_of_matrix(k, prev):
            bk = binv[k]
            mhi, mlo = split(bk * rate_of(k))
            qhi, qlo = split(prev)
            new = mm3(mhi, mlo, qhi, qlo)
            both = jnp.concatenate([bk, bk], axis=1)
            both = jnp.concatenate([both] * (wide // (2 * classes)), axis=1)
            new = new + jnp.where(lax.div(lane, classes) == k, both, 0.0)
            nhi, nlo = split(new)
            phi[pl.ds(pl.multiple_of(k * classes, classes), classes)] = nhi
            plo[pl.ds(pl.multiple_of(k * classes, classes), classes)] = nlo
            return new

        early = CHUNKS // 4
        for ch in range(early):
            lo, hi = levels * ch // early, levels * (ch + 1) // early
            prev = lax.fori_loop(lo, hi, level_of_matrix, prev)
            arrive(ch)

        @pl.when(has_adj)
        def _():
            adj_copy.wait_recv()

        build(g_adj, info_adj, adj)

        def gather(src, first, g, r):
            out = jnp.zeros((block, cols), F32)
            for b in range(3):
                hi, lo = split(src[first + b, r])
                gb = g[b * cols:(b + 1) * cols]
                out = out + mm(hi, gb) + mm(lo, gb)
            return out

        def put_x(r, s, value):
            hi, lo = split(value)
            xhi[r, s * cols:(s + 1) * cols] = hi
            xlo[r, s * cols:(s + 1) * cols] = lo

        tail = slice(rows - classes, rows)
        ti = slice(rows, rows + classes)
        n_blocks = rows // block

        def first_sums(b):
            r = slice(b * block, (b + 1) * block)
            value = gather(win, own - 1, g_own, r)
            h1[1, r] = value
            put_x(r, 0, win[own, r])
            put_x(r, 1, value)
            h_copy[b].start()
            h1[2 * c, r] = gather(win, c, g_adj, r)

        def sweep_block(b, x_cols, buf):
            r = slice(b * block, (b + 1) * block)
            k = slice(0, (b + 1) * block)
            buf[classes + b * block:classes + (b + 1) * block] = mm3(
                phi[r, k], plo[r, k], xhi[k, :x_cols], xlo[k, :x_cols])

        def second_sums(b):
            r = slice(b * block, (b + 1) * block)
            h_copy[b].wait_recv()
            put_x(r, 2, gather(h1, 0, g_own, r))
            sweep_block(b, 3 * cols, fbuf)

        h_copy = []
        for b in range(n_blocks):
            r = pl.ds(b * block, block)
            h_copy.append(remote(h1.at[1, r], h1.at[2 * c, r], h_s.at[b], h_r.at[b],
                                 {"horiz": mate}))
        per = CHUNKS // n_blocks
        for b in range(n_blocks):
            for ch in range(b * per, (b + 1) * per):
                remote(piece(mate_pos, ch), piece(mate_pos, ch), send_mate.at[ch],
                       recv.at[mate_pos, ch], {"horiz": mate}).wait_recv()
                if ch >= early:
                    arrive(ch)
            first_sums(b)
            if b > 0:
                second_sums(b - 1)
        second_sums(n_blocks - 1)

        def relay(buf, out, up_cols, sem, rest):
            down = remote(out, buf.at[0:classes], v_s.at[sem], v_r.at[sem], {"vert": v + 1})
            up = remote(buf.at[classes:2 * classes, 0:up_cols],
                        buf.at[classes + rows:2 * classes + rows, 0:up_cols],
                        v_s.at[sem + 1], v_r.at[sem + 1], {"vert": v - 1})
            out[...] = buf[rows:rows + classes]

            @pl.when(jnp.logical_and(first_slab, slabs > 1))
            def _():
                down.start()

            rest()

            @pl.when(jnp.logical_not(first_slab))
            def _():
                down.wait_recv()
                ihi, ilo = split(buf[0:classes])
                out[...] = out[...] + mm3(phi[tail, ti], plo[tail, ti], ihi, ilo)

                @pl.when(jnp.logical_not(last_slab))
                def _():
                    down.start()

                for b in range(n_blocks):
                    r = slice(b * block, (b + 1) * block)
                    br = slice(classes + b * block, classes + (b + 1) * block)
                    buf[br] = buf[br] + mm3(phi[r, ti], plo[r, ti], ihi, ilo)
                    if b == 0:
                        up.start()

            def finish():
                @pl.when(jnp.logical_not(last_slab))
                def _():
                    up.wait_recv()
                    down.wait_send()

                @pl.when(jnp.logical_not(first_slab))
                def _():
                    up.wait_send()

            return finish

        def operate(k, buf, width):
            at = k * classes if isinstance(k, int) else pl.multiple_of(k * classes, classes)
            here = buf[pl.ds(at + classes, classes), 0:width]
            above = buf[pl.ds(at, classes), 0:width]
            below = buf[pl.ds(at + 2 * classes, classes), 0:width]
            chi, clo = split(coup[k])
            hhi, hlo = split(here)
            d = column(diag_of(k))
            ra = column(rate_of(k))
            return (d * here + mm3(chi, clo, hhi, hlo) - ra * above - VERT_DIFFUSION * below)

        finish_f = relay(fbuf, fout, 2 * cols, 0, lambda: None)

        def level_rows(k, more):
            at = (k + more) * classes
            return pl.ds(at if isinstance(k, int) else pl.multiple_of(at, classes), classes)

        def middle(k, carry):
            r = level_rows(k, 0)
            rf = level_rows(k, 1)
            lf = operate(k, fbuf, 2 * cols)
            m = win[own, r] - lf[:, :cols] + HORIZ_DIFFUSION * fbuf[rf, cols:2 * cols]
            hm = h1[1, r] - lf[:, cols:] + HORIZ_DIFFUSION * fbuf[rf, 2 * cols:3 * cols]
            mid[r] = m
            put_x(r, 0, m)
            put_x(r, 1, hm)
            return carry

        def middles(i, carry):
            for u in range(4):
                middle(4 * i + u, carry)
            return carry

        lax.fori_loop(0, levels // 4 - 1, middles, 0)
        finish_f()
        middles(levels // 4 - 1, 0)
        sweep_block(n_blocks - 1, 2 * cols, pbuf)

        def others():
            for b in range(n_blocks - 1):
                sweep_block(b, 2 * cols, pbuf)

        finish_p = relay(pbuf, pout, cols, 2, others)
        upper = slice(0, classes + rows)
        below_row = slice(classes + rows, 2 * classes + rows)
        sbuf[upper] = CA * fbuf[upper, 0:cols] + CB * pbuf[upper, 0:cols]

        def final(k, carry):
            r = level_rows(k, 0)
            rf = level_rows(k, 1)
            hs = CA * fbuf[rf, cols:2 * cols] + CB * pbuf[rf, cols:2 * cols]
            sol[r] = fbuf[rf, 0:cols] + sbuf[rf]
            res[r] = mid[r] - operate(k, sbuf, cols) + HORIZ_DIFFUSION * hs
            return carry

        def finals(i, carry):
            for u in range(4):
                final(4 * i + u, carry)
            return carry

        lax.fori_loop(0, levels // 4 - 1, finals, 0)
        finish_p()
        sbuf[below_row] = CA * fbuf[below_row, 0:cols] + CB * pbuf[below_row, 0:cols]
        finals(levels // 4 - 1, 0)

        for cp in directs + mates:
            cp.wait_send()
        for cp in h_copy:
            cp.wait_send()

        @pl.when(has_adj)
        def _():
            adj_copy.wait_send()

        @pl.when(has_fwd)
        def _():
            for ch in range(CHUNKS):
                for i in range(2):
                    fwd_copy(i, ch).wait_send()

    return kernel


def solution(mesh):
    tiles, slabs = mesh.shape["horiz"], mesh.shape["vert"]

    def body(right_side, neighbours, ocean_count, settling, coupling, precond_inverse):
        levels, classes, cols = right_side.shape
        rows = levels * classes
        vm = pl.BlockSpec(memory_space=pltpu.VMEM)
        dma = pltpu.SemaphoreType.DMA
        wide = rows + 2 * classes
        sol, res = pl.pallas_call(
            make_kernel(tiles, slabs, levels, classes, cols),
            out_shape=[jax.ShapeDtypeStruct((rows, cols), F32)] * 2,
            in_specs=[vm, vm, pl.BlockSpec(memory_space=pltpu.SMEM)] + [vm] * 3,
            out_specs=[vm, vm],
            scratch_shapes=[
                pltpu.VMEM((4, rows, cols), F32),
                pltpu.VMEM((8, cols), jnp.int32),
                pltpu.VMEM((8, cols), jnp.int32),
                pltpu.VMEM((3, rows, cols), F32),
                pltpu.VMEM((3 * cols, cols), BF),
                pltpu.VMEM((3 * cols, cols), BF),
                pltpu.VMEM((rows, wide), BF),
                pltpu.VMEM((rows, wide), BF),
                pltpu.VMEM((rows, 3 * cols), BF),
                pltpu.VMEM((rows, 3 * cols), BF),
                pltpu.VMEM((rows + 2 * classes, 3 * cols), F32),
                pltpu.VMEM((classes, 3 * cols), F32),
                pltpu.VMEM((rows, cols), F32),
                pltpu.VMEM((rows + 2 * classes, 2 * cols), F32),
                pltpu.VMEM((classes, 2 * cols), F32),
                pltpu.VMEM((rows + 2 * classes, cols), F32),
                dma((4, CHUNKS)), dma((CHUNKS,)), dma((CHUNKS,)), dma((2, CHUNKS)),
                dma, dma, dma((4,)), dma((4,)), dma((4,)), dma((4,)),
            ],
            compiler_params=pltpu.CompilerParams(
                collective_id=0, has_side_effects=True, vmem_limit_bytes=56 * 2**20),
            name="settle",
        )(right_side.reshape(rows, cols), neighbours, ocean_count, settling, coupling,
          precond_inverse)
        return sol.reshape(right_side.shape), res.reshape(right_side.shape)

    in_specs = (P("vert", None, "horiz"), P(None, "horiz"), P("horiz"), P(),
                P("vert", None, None), P("vert", None, None))
    out_specs = (P("vert", None, "horiz"), P("vert", None, "horiz"))
    return jax.shard_map(body, mesh=mesh, in_specs=in_specs, out_specs=out_specs, check_vma=False)
```

```python
import jax
import jax.numpy as jnp
from jax import lax
from jax.experimental import pallas as pl
from jax.experimental.pallas import tpu as pltpu
from jax.sharding import PartitionSpec as P

VERT_DIFFUSION = 0.5
HORIZ_DIFFUSION = 0.25
HALF_WIDTH = 0.6
NB = 4
SPREAD = 1.0 / HALF_WIDTH
RATIO_FIRST = 1.0 / SPREAD
RATIO_SECOND = 1.0 / (2.0 * SPREAD - RATIO_FIRST)
CA = RATIO_SECOND * RATIO_FIRST
CB = 2.0 * RATIO_SECOND / HALF_WIDTH

F32 = jnp.float32
BF = jnp.bfloat16
CHUNKS = 16


def split(x):
    hi = x.astype(BF)
    return hi, (x - hi.astype(F32)).astype(BF)


def mm(a, b):
    return jnp.dot(a, b, preferred_element_type=F32)


def mm3(ahi, alo, bhi, blo):
    return mm(ahi, bhi) + mm(ahi, blo) + mm(alo, bhi)


def make_kernel(tiles, slabs, levels, classes, cols):
    rows = levels * classes
    part = rows // CHUNKS
    block = 256

    def kernel(rhs, nbr, count, settling, coup, binv, sol, res,
               win, info, info_adj, h1, g_own, g_adj, phi, plo, xhi, xlo, fbuf, fout, mid,
               pbuf, pout, sbuf,
               recv, send_mate, send_direct, send_fwd, info_s, info_r, h_s, h_r, v_s, v_r):
        t = lax.axis_index("horiz")
        v = lax.axis_index("vert")
        c = lax.rem(t, 2)
        j = lax.div(t, 2)
        odd = lax.rem(j, 2)
        inner = lax.rem(j + c, 2) == 1
        own = 2 - c
        mate_pos = 3 - 3 * c
        mate = t + 1 - 2 * c
        direct = jnp.where(odd == 0, 2 * j + 2, 2 * j - 1)
        fwd = jnp.where(odd == 0, 2 * j + 4, 2 * j - 3)
        has_fwd = jnp.logical_and(inner, jnp.logical_and(fwd >= 0, fwd < tiles))
        adj = t - 1 + 2 * c
        has_adj = jnp.logical_and(adj >= 0, adj < tiles)
        first_slab = v == 0
        last_slab = v == slabs - 1

        def remote(src, dst, s, r, to):
            return pltpu.make_async_remote_copy(
                src_ref=src, dst_ref=dst, send_sem=s, recv_sem=r, device_id=to,
                device_id_type=pl.DeviceIdType.MESH)

        def piece(pos, ch):
            return win.at[pos, pl.ds(ch * part, part)]

        pj = j + 1 - 2 * odd
        partner_inner = direct
        partner_outer = 4 * pj + 1 - direct
        outer = jnp.logical_not(inner)
        from_fwd = jnp.where(odd == 0, 2 * j - 3, 2 * j + 4)
        outer_adj = jnp.logical_and(outer, has_adj)
        barrier = pltpu.get_barrier_semaphore()

        def greet(to):
            pl.semaphore_signal(barrier, inc=1, device_id=to, device_id_type=pl.DeviceIdType.MESH)

        greet({"horiz": mate})
        greet({"horiz": partner_inner})

        @pl.when(inner)
        def _():
            greet({"horiz": partner_outer})

        @pl.when(has_fwd)
        def _():
            greet({"horiz": fwd})

        @pl.when(outer_adj)
        def _():
            greet({"horiz": from_fwd})
            greet({"horiz": adj})

        @pl.when(jnp.logical_not(first_slab))
        def _():
            greet({"vert": v - 1})

        @pl.when(jnp.logical_not(last_slab))
        def _():
            greet({"vert": v + 1})

        greeted = (2 + jnp.where(inner, 1, 0) + jnp.where(has_fwd, 1, 0)
                   + jnp.where(outer_adj, 2, 0) + jnp.where(first_slab, 0, 1)
                   + jnp.where(last_slab, 0, 1))

        inside = lax.broadcasted_iota(jnp.int32, (1, cols), 1)
        n = count[0]
        low = lax.div(n + 1, 2)
        high = cols - lax.div(n, 2)
        ocean = jnp.logical_or(inside < low, inside >= high)
        ocean_i = ocean.astype(jnp.int32)
        ocean_f = ocean.astype(F32)
        info[...] = jnp.concatenate([nbr[...], jnp.broadcast_to(ocean_i, (4, cols))], axis=0)
        for ch in range(CHUNKS):
            r = pl.ds(ch * part, part)
            win[own, r] = rhs[r] * ocean_f
        pl.semaphore_wait(barrier, greeted)
        adj_copy = remote(info, info_adj, info_s, info_r, {"horiz": adj})

        @pl.when(has_adj)
        def _():
            adj_copy.start()

        directs = []
        for ch in range(CHUNKS):
            cp = remote(piece(own, ch), piece(c + 2 * odd, ch), send_direct.at[ch],
                        recv.at[c + 2 * odd, ch], {"horiz": direct})
            cp.start()
            directs.append(cp)
        mates = []
        for ch in range(CHUNKS):
            cp = remote(piece(own, ch), piece(3 * c, ch), send_mate.at[ch],
                        recv.at[3 * c, ch], {"horiz": mate})
            cp.start()
            mates.append(cp)

        @pl.when(jnp.logical_not(has_adj))
        def _():
            info_adj[...] = jnp.zeros_like(info_adj)
            win[2 * c] = jnp.zeros((rows, cols), F32)
            win[2 * c + 1] = jnp.zeros((rows, cols), F32)

        @pl.when(first_slab)
        def _():
            fbuf[0:classes] = jnp.zeros((classes, 3 * cols), F32)
            pbuf[0:classes] = jnp.zeros((classes, 2 * cols), F32)

        @pl.when(last_slab)
        def _():
            fbuf[classes + rows:] = jnp.zeros((classes, 3 * cols), F32)
            pbuf[classes + rows:] = jnp.zeros((classes, 2 * cols), F32)

        def fwd_copy(i, ch):
            return remote(piece(2 * c + i, ch), piece(2 * (1 - c) + i, ch), send_fwd.at[i, ch],
                          recv.at[2 * (1 - c) + i, ch], {"horiz": fwd})

        def arrive(ch):
            for i in range(2):
                @pl.when(has_adj)
                def _():
                    remote(piece(2 * c + i, ch), piece(2 * c + i, ch), send_fwd.at[i, ch],
                           recv.at[2 * c + i, ch], {"horiz": mate}).wait_recv()

                @pl.when(has_fwd)
                def _():
                    fwd_copy(i, ch).start()

        def build(dst, source, tile):
            base = (tile - 1) * cols
            mask = source[4:5].astype(F32)
            for b in range(3):
                at = lax.broadcasted_iota(jnp.int32, (cols, cols), 0) + (base + b * cols)
                total = jnp.zeros((cols, cols), F32)
                for q in range(NB):
                    total = total + jnp.where(at == source[q:q + 1], 1.0, 0.0)
                dst[b * cols:(b + 1) * cols] = (total * mask).astype(BF)

        build(g_own, info, t)

        eye = (lax.broadcasted_iota(jnp.int32, (classes, classes), 0)
               == lax.broadcasted_iota(jnp.int32, (classes, classes), 1))

        def rate_of(k):
            level = v * levels + k
            above = settling[pl.ds(jnp.maximum(level - 1, 0), 1)]
            return jnp.where(level > 0, above, 0.0) + VERT_DIFFUSION

        def diag_of(k):
            return (1.0 + settling[pl.ds(v * levels + k, 1)] + 2.0 * VERT_DIFFUSION
                    + NB * HORIZ_DIFFUSION)

        def column(x):
            return jnp.sum(jnp.where(eye, x, 0.0), axis=1, keepdims=True)

        wide = rows + 2 * classes
        lane = lax.broadcasted_iota(jnp.int32, (classes, wide), 1)
        row = lax.broadcasted_iota(jnp.int32, (classes, wide), 0)
        prev = jnp.where(lane == row + rows, 1.0, 0.0)

        def level_of_matrix(k, prev):
            bk = binv[k]
            mhi, mlo = split(bk * rate_of(k))
            qhi, qlo = split(prev)
            new = mm3(mhi, mlo, qhi, qlo)
            both = jnp.concatenate([bk, bk], axis=1)
            both = jnp.concatenate([both] * (wide // (2 * classes)), axis=1)
            new = new + jnp.where(lax.div(lane, classes) == k, both, 0.0)
            nhi, nlo = split(new)
            phi[pl.ds(pl.multiple_of(k * classes, classes), classes)] = nhi
            plo[pl.ds(pl.multiple_of(k * classes, classes), classes)] = nlo
            return new

        early = CHUNKS // 4
        for ch in range(early):
            lo, hi = levels * ch // early, levels * (ch + 1) // early
            prev = lax.fori_loop(lo, hi, level_of_matrix, prev)
            arrive(ch)

        @pl.when(has_adj)
        def _():
            adj_copy.wait_recv()

        build(g_adj, info_adj, adj)

        def gather(src, first, g, r):
            out = jnp.zeros((block, cols), F32)
            for b in range(3):
                hi, lo = split(src[first + b, r])
                gb = g[b * cols:(b + 1) * cols]
                out = out + mm(hi, gb) + mm(lo, gb)
            return out

        def put_x(r, s, value):
            hi, lo = split(value)
            xhi[r, s * cols:(s + 1) * cols] = hi
            xlo[r, s * cols:(s + 1) * cols] = lo

        tail = slice(rows - classes, rows)
        ti = slice(rows, rows + classes)
        n_blocks = rows // block

        def first_sums(b):
            r = slice(b * block, (b + 1) * block)
            value = gather(win, own - 1, g_own, r)
            h1[1, r] = value
            put_x(r, 0, win[own, r])
            put_x(r, 1, value)
            h_copy[b].start()
            h1[2 * c, r] = gather(win, c, g_adj, r)

        def sweep_block(b, x_cols, buf, from_col=0):
            r = slice(b * block, (b + 1) * block)
            k = slice(0, (b + 1) * block)
            w = slice(from_col, x_cols)
            buf[classes + b * block:classes + (b + 1) * block, w] = mm3(
                phi[r, k], plo[r, k], xhi[k, w], xlo[k, w])

        def second_sums(b):
            r = slice(b * block, (b + 1) * block)
            sweep_block(b, 2 * cols, fbuf)
            h_copy[b].wait_recv()
            put_x(r, 2, gather(h1, 0, g_own, r))
            sweep_block(b, 3 * cols, fbuf, 2 * cols)

        h_copy = []
        for b in range(n_blocks):
            r = pl.ds(b * block, block)
            h_copy.append(remote(h1.at[1, r], h1.at[2 * c, r], h_s.at[b], h_r.at[b],
                                 {"horiz": mate}))
        per = CHUNKS // n_blocks
        for b in range(n_blocks):
            for ch in range(b * per, (b + 1) * per):
                remote(piece(mate_pos, ch), piece(mate_pos, ch), send_mate.at[ch],
                       recv.at[mate_pos, ch], {"horiz": mate}).wait_recv()
                if ch >= early:
                    arrive(ch)
            first_sums(b)
            if b > 0:
                second_sums(b - 1)
        second_sums(n_blocks - 1)

        def relay(buf, out, up_cols, sem, rest):
            down = remote(out, buf.at[0:classes], v_s.at[sem], v_r.at[sem], {"vert": v + 1})
            up = remote(buf.at[classes:2 * classes, 0:up_cols],
                        buf.at[classes + rows:2 * classes + rows, 0:up_cols],
                        v_s.at[sem + 1], v_r.at[sem + 1], {"vert": v - 1})
            out[...] = buf[rows:rows + classes]

            @pl.when(jnp.logical_and(first_slab, slabs > 1))
            def _():
                down.start()

            rest()

            @pl.when(jnp.logical_not(first_slab))
            def _():
                down.wait_recv()
                ihi, ilo = split(buf[0:classes])
                out[...] = out[...] + mm3(phi[tail, ti], plo[tail, ti], ihi, ilo)

                @pl.when(jnp.logical_not(last_slab))
                def _():
                    down.start()

                for b in range(n_blocks):
                    r = slice(b * block, (b + 1) * block)
                    br = slice(classes + b * block, classes + (b + 1) * block)
                    buf[br] = buf[br] + mm3(phi[r, ti], plo[r, ti], ihi, ilo)
                    if b == 0:
                        up.start()

            def finish():
                @pl.when(jnp.logical_not(last_slab))
                def _():
                    up.wait_recv()
                    down.wait_send()

                @pl.when(jnp.logical_not(first_slab))
                def _():
                    up.wait_send()

            return finish

        def operate(k, buf, width):
            at = k * classes if isinstance(k, int) else pl.multiple_of(k * classes, classes)
            here = buf[pl.ds(at + classes, classes), 0:width]
            above = buf[pl.ds(at, classes), 0:width]
            below = buf[pl.ds(at + 2 * classes, classes), 0:width]
            chi, clo = split(coup[k])
            hhi, hlo = split(here)
            d = column(diag_of(k))
            ra = column(rate_of(k))
            return (d * here + mm3(chi, clo, hhi, hlo) - ra * above - VERT_DIFFUSION * below)

        finish_f = relay(fbuf, fout, 2 * cols, 0, lambda: None)

        def level_rows(k, more):
            at = (k + more) * classes
            return pl.ds(at if isinstance(k, int) else pl.multiple_of(at, classes), classes)

        def middle(k, carry):
            r = level_rows(k, 0)
            rf = level_rows(k, 1)
            lf = operate(k, fbuf, 2 * cols)
            m = win[own, r] - lf[:, :cols] + HORIZ_DIFFUSION * fbuf[rf, cols:2 * cols]
            hm = h1[1, r] - lf[:, cols:] + HORIZ_DIFFUSION * fbuf[rf, 2 * cols:3 * cols]
            mid[r] = m
            put_x(r, 0, m)
            put_x(r, 1, hm)
            return carry

        def middles(i, carry):
            for u in range(4):
                middle(4 * i + u, carry)
            return carry

        lax.fori_loop(0, levels // 4 - 1, middles, 0)
        finish_f()
        middles(levels // 4 - 1, 0)
        sweep_block(n_blocks - 1, 2 * cols, pbuf)

        def others():
            for b in range(n_blocks - 1):
                sweep_block(b, 2 * cols, pbuf)

        finish_p = relay(pbuf, pout, cols, 2, others)
        upper = slice(0, classes + rows)
        below_row = slice(classes + rows, 2 * classes + rows)
        sbuf[upper] = CA * fbuf[upper, 0:cols] + CB * pbuf[upper, 0:cols]

        def final(k, carry):
            r = level_rows(k, 0)
            rf = level_rows(k, 1)
            hs = CA * fbuf[rf, cols:2 * cols] + CB * pbuf[rf, cols:2 * cols]
            sol[r] = fbuf[rf, 0:cols] + sbuf[rf]
            res[r] = mid[r] - operate(k, sbuf, cols) + HORIZ_DIFFUSION * hs
            return carry

        def finals(i, carry):
            for u in range(4):
                final(4 * i + u, carry)
            return carry

        lax.fori_loop(0, levels // 4 - 1, finals, 0)
        finish_p()
        sbuf[below_row] = CA * fbuf[below_row, 0:cols] + CB * pbuf[below_row, 0:cols]
        finals(levels // 4 - 1, 0)

        for cp in directs + mates:
            cp.wait_send()
        for cp in h_copy:
            cp.wait_send()

        @pl.when(has_adj)
        def _():
            adj_copy.wait_send()

        @pl.when(has_fwd)
        def _():
            for ch in range(CHUNKS):
                for i in range(2):
                    fwd_copy(i, ch).wait_send()

    return kernel


def solution(mesh):
    tiles, slabs = mesh.shape["horiz"], mesh.shape["vert"]

    def body(right_side, neighbours, ocean_count, settling, coupling, precond_inverse):
        levels, classes, cols = right_side.shape
        rows = levels * classes
        vm = pl.BlockSpec(memory_space=pltpu.VMEM)
        dma = pltpu.SemaphoreType.DMA
        wide = rows + 2 * classes
        sol, res = pl.pallas_call(
            make_kernel(tiles, slabs, levels, classes, cols),
            out_shape=[jax.ShapeDtypeStruct((rows, cols), F32)] * 2,
            in_specs=[vm, vm, pl.BlockSpec(memory_space=pltpu.SMEM)] + [vm] * 3,
            out_specs=[vm, vm],
            scratch_shapes=[
                pltpu.VMEM((4, rows, cols), F32),
                pltpu.VMEM((8, cols), jnp.int32),
                pltpu.VMEM((8, cols), jnp.int32),
                pltpu.VMEM((3, rows, cols), F32),
                pltpu.VMEM((3 * cols, cols), BF),
                pltpu.VMEM((3 * cols, cols), BF),
                pltpu.VMEM((rows, wide), BF),
                pltpu.VMEM((rows, wide), BF),
                pltpu.VMEM((rows, 3 * cols), BF),
                pltpu.VMEM((rows, 3 * cols), BF),
                pltpu.VMEM((rows + 2 * classes, 3 * cols), F32),
                pltpu.VMEM((classes, 3 * cols), F32),
                pltpu.VMEM((rows, cols), F32),
                pltpu.VMEM((rows + 2 * classes, 2 * cols), F32),
                pltpu.VMEM((classes, 2 * cols), F32),
                pltpu.VMEM((rows + 2 * classes, cols), F32),
                dma((4, CHUNKS)), dma((CHUNKS,)), dma((CHUNKS,)), dma((2, CHUNKS)),
                dma, dma, dma((4,)), dma((4,)), dma((4,)), dma((4,)),
            ],
            compiler_params=pltpu.CompilerParams(
                collective_id=0, has_side_effects=True, vmem_limit_bytes=56 * 2**20),
            name="settle",
        )(right_side.reshape(rows, cols), neighbours, ocean_count, settling, coupling,
          precond_inverse)
        return sol.reshape(right_side.shape), res.reshape(right_side.shape)

    in_specs = (P("vert", None, "horiz"), P(None, "horiz"), P("horiz"), P(),
                P("vert", None, None), P("vert", None, None))
    out_specs = (P("vert", None, "horiz"), P("vert", None, "horiz"))
    return jax.shard_map(body, mesh=mesh, in_specs=in_specs, out_specs=out_specs, check_vma=False)
```
